256 devices in a mesh: ctx: 16 (over z, core), tp: 4 (over y), dp: 4 (over x).
Axes of the slice: x: 4, y: 4, z: 8, core: 2. Of those that a mesh axis runs over, the one named last changes fastest.
Arguments:
- queries: bfloat16 [49152, 4096], P(('dp', 'ctx'), 'tp'), parts along dimension 0, may hold values from -6 to 6
- key_vectors: bfloat16 [49152, 4096], P(('dp', 'ctx'), 'tp'), parts along dimension 0, may hold values from -6 to 6
- value_vectors: bfloat16 [49152, 4096], P(('dp', 'ctx'), 'tp'), parts along dimension 0, may hold values from -6 to 6
- out_grad: bfloat16 [49152, 4096], P(('dp', 'ctx'), 'tp'), parts along dimension 0, may hold values from -6 to 6
Outputs:
- grad_queries: bfloat16 [49152, 4096], P(('dp', 'ctx'), 'tp'), parts along dimension 0
- grad_keys: bfloat16 [49152, 4096], P(('dp', 'ctx'), 'tp'), parts along dimension 0
- grad_values: bfloat16 [49152, 4096], P(('dp', 'ctx'), 'tp'), parts along dimension 0
The draws below stay inside these ranges and needn't reach their ends.
There are 4 independent parts, one for each index of `dp`. The reference program is written for one: setup_inputs(seed, part) draws one part's arguments, and reference() takes and returns one part's arrays. A program takes and returns all parts, laid end to end along the dimension named above; each array names one. Nothing has to cross between parts.
All inputs are finite; a program needn't handle non-finite values.
Results may differ from the reference program's by a relative error of at most 0.014.
Values may be sent and summed in bfloat16 or wider, within the bound.
No kernel may reach another device: no remote copies, remote signals or barrier semaphores. Data moves between devices by JAX's collectives and lax.ppermute only.
A program may use at most 128 MiB of HBM per device.

```python
import math
import jax
import jax.numpy as jnp
from jax import lax

HEAD = 128
HEADS = 32
TOK_DEV = 768
LENGTH = 12288
N_CTX = 16


def block_scale(rng, shape, shards, least, top_value):
    def one(axis_at, blocks):
        heights = jax.random.uniform(jax.random.fold_in(jax.random.fold_in(rng, 6), axis_at), (blocks,), jnp.float32, least / len(shards), top_value / len(shards))
        return jnp.repeat(jnp.exp(heights), shape[axis_at] // blocks).reshape((-1,) + (1,) * (len(shape) - axis_at - 1))

    gain = one(*shards[0])
    for cut in shards[1:]:
        gain = gain * one(*cut)
    return gain


def bell_draw(rng, extent, deviation, reach, shards=(), held_as=jnp.bfloat16):
    factor_of = block_scale(rng, extent, shards, -0.22, 0.18) if shards else 1.0
    drawn = jax.random.normal(rng, extent, jnp.float32) * deviation * factor_of
    return jnp.minimum(jnp.maximum(drawn, -reach), reach).astype(held_as)


def setup_inputs(seed: int = 0, part: int = 0) -> dict:
    seeds = jax.random.split(jax.random.key(seed), 5)
    part_splits = jax.random.split(jax.random.fold_in(seeds[4], part), 5)
    queries = bell_draw(part_splits[0], (LENGTH, HEADS * HEAD), 1.0, 6.0, ((0, 16), (1, 4)))
    key_vectors = bell_draw(part_splits[1], (LENGTH, HEADS * HEAD), 1.0, 6.0, ((0, 16), (1, 4)))
    value_vectors = bell_draw(part_splits[2], (LENGTH, HEADS * HEAD), 1.0, 6.0, ((0, 16), (1, 4)))
    out_grad = bell_draw(part_splits[3], (LENGTH, HEADS * HEAD), 1.0, 6.0, ((0, 16), (1, 4)))
    return dict(queries=queries, key_vectors=key_vectors, value_vectors=value_vectors, out_grad=out_grad)


def head_block(query_rows, key_rows, value_rows, grad_rows, prefix_low, suffix_low, factor):
    count_rows = query_rows.shape[0]
    causal = lax.broadcasted_iota(jnp.int32, (count_rows, count_rows), 0) >= lax.broadcasted_iota(jnp.int32, (count_rows, count_rows), 1)
    scores = jnp.dot(query_rows, key_rows.T, preferred_element_type=jnp.float32)
    weights = jnp.where(causal, factor * scores, 0.0).astype(jnp.bfloat16)
    upstream = jnp.where(causal, factor * jnp.dot(grad_rows, value_rows.T, preferred_element_type=jnp.float32), 0.0).astype(jnp.bfloat16)
    grad_query = jnp.dot(upstream, key_rows, preferred_element_type=jnp.float32) + jnp.dot(grad_rows, prefix_low.T, preferred_element_type=jnp.float32)
    grad_key = jnp.dot(upstream.T, query_rows, preferred_element_type=jnp.float32) + jnp.dot(value_rows, suffix_low.T, preferred_element_type=jnp.float32)
    grad_value = jnp.dot(weights.T, grad_rows, preferred_element_type=jnp.float32) + jnp.dot(key_rows, suffix_low, preferred_element_type=jnp.float32)
    return (grad_query.astype(jnp.bfloat16), grad_key.astype(jnp.bfloat16), grad_value.astype(jnp.bfloat16))

def reference(queries, key_vectors, value_vectors, out_grad):
    factor = 1.0 / math.sqrt(HEAD * LENGTH)

    def blocked(matrix_in):
        return matrix_in.reshape(N_CTX, TOK_DEV, HEADS, HEAD).transpose(0, 2, 1, 3)
    query_blocks = blocked(queries)
    key_blocks = blocked(key_vectors)
    value_blocks = blocked(value_vectors)
    grad_blocks = blocked(out_grad)
    local_state = (factor * jnp.einsum('nhti,nhtj->nhij', key_blocks.astype(jnp.float32), value_blocks.astype(jnp.float32))).astype(jnp.bfloat16)
    local_grad = (factor * jnp.einsum('nhti,nhtj->nhij', query_blocks.astype(jnp.float32), grad_blocks.astype(jnp.float32))).astype(jnp.bfloat16)
    wide_state = local_state.astype(jnp.float32)
    wide_grad = local_grad.astype(jnp.float32)
    empty_state = jnp.zeros_like(wide_state[:1])
    prefix = jnp.concatenate([empty_state, jnp.cumsum(wide_state, 0)[:-1]], 0)
    backward_sums = jnp.cumsum(wide_grad[::-1], 0)[::-1]
    suffix = jnp.concatenate([backward_sums[1:], empty_state], 0)
    prefix_low = prefix.astype(jnp.bfloat16)
    suffix_low = suffix.astype(jnp.bfloat16)

    def one_block(operands):
        return jax.vmap(lambda a, b, c, d, e, f: head_block(a, b, c, d, e, f, factor))(*operands)
    grad_query, grad_key, grad_value = lax.map(one_block, (query_blocks, key_blocks, value_blocks, grad_blocks, prefix_low, suffix_low))

    def unblocked(tensor_in):
        return tensor_in.transpose(0, 2, 1, 3).reshape(LENGTH, HEADS * HEAD)
    return (unblocked(grad_query), unblocked(grad_key), unblocked(grad_value))
```

```python
import math

import jax
import jax.numpy as jnp
from jax import lax
from jax.experimental import pallas as pl
from jax.experimental.pallas import tpu as pltpu
from jax.sharding import PartitionSpec as P

HEAD = 128
SUB = 256
PAIR = 2 * HEAD
F32 = jnp.float32
BF16 = jnp.bfloat16

NN = (((1,), (0,)), ((), ()))
NT = (((1,), (1,)), ((), ()))
TN = (((0,), (0,)), ((), ()))


def mm(a, b, dims):
    return lax.dot_general(a, b, dims, preferred_element_type=F32)


def states_kernel(factor, q_ref, k_ref, v_ref, g_ref, state_ref, local_ref):
    subs = q_ref.shape[0] // SUB
    for head in range(2):
        cols = slice(head * HEAD, (head + 1) * HEAD)
        for kind, (left, right) in enumerate(((k_ref, v_ref), (q_ref, g_ref))):
            parts = []
            for sub in range(subs):
                rows = slice(sub * SUB, (sub + 1) * SUB)
                parts.append(factor * mm(left[rows, cols], right[rows, cols], TN))
            if kind == 1:
                parts = parts[::-1]
            total = parts[0]
            for sub in range(1, subs):
                local_ref[kind, head, sub - 1] = total.astype(BF16)
                total = total + parts[sub]
            state_ref[kind, head] = total.astype(BF16)


def intra_kernel(factor, q_ref, k_ref, v_ref, g_ref, gq_ref, gk_ref, gv_ref):
    row = lax.broadcasted_iota(jnp.int32, (SUB, SUB), 0)
    col = lax.broadcasted_iota(jnp.int32, (SUB, SUB), 1)
    subs = q_ref.shape[0] // SUB
    for head in range(2):
        cols = slice(head * HEAD, (head + 1) * HEAD)
        for sub in range(subs):
            rows = slice(sub * SUB, (sub + 1) * SUB)
            q, k, v, g = (ref[rows, cols] for ref in (q_ref, k_ref, v_ref, g_ref))
            weights_t = jnp.where(col >= row, factor * mm(k, q, NT), 0.0).astype(BF16)
            upstream = jnp.where(row >= col, factor * mm(g, v, NT), 0.0).astype(BF16)
            gq_ref[rows, cols] = mm(upstream, k, NN).astype(BF16)
            gk_ref[rows, cols] = mm(upstream, q, TN).astype(BF16)
            gv_ref[rows, cols] = mm(weights_t, g, NN).astype(BF16)


def block_diagonal(first, second):
    zero = jnp.zeros_like(first)
    return jnp.concatenate(
        [jnp.concatenate([first, zero], 1), jnp.concatenate([zero, second], 1)], 0
    )


def final_kernel(
    k_ref, v_ref, g_ref, gq_in, gk_in, gv_in, prefix_ref, suffix_ref, local_ref, gq_ref, gk_ref, gv_ref
):
    subs = k_ref.shape[0] // SUB

    def of_sub(wide_ref, kind, count):
        heads = []
        for head in range(2):
            wide = wide_ref[head]
            if count > 0:
                wide = wide.astype(F32) + local_ref[kind, head, count - 1].astype(F32)
            heads.append(wide.astype(BF16))
        return block_diagonal(*heads)

    for sub in range(subs):
        rows = slice(sub * SUB, (sub + 1) * SUB)
        prefix = of_sub(prefix_ref, 0, sub)
        suffix = of_sub(suffix_ref, 1, subs - 1 - sub)
        gq_ref[rows, :] = (gq_in[rows, :].astype(F32) + mm(g_ref[rows, :], prefix, NT)).astype(BF16)
        gk_ref[rows, :] = (gk_in[rows, :].astype(F32) + mm(v_ref[rows, :], suffix, NT)).astype(BF16)
        gv_ref[rows, :] = (gv_in[rows, :].astype(F32) + mm(k_ref[rows, :], suffix, NN)).astype(BF16)


def on_device(queries, key_vectors, value_vectors, out_grad):
    rows, width = queries.shape
    heads = width // HEAD
    pairs = heads // 2
    half = heads // 2
    count_ctx = lax.axis_size("ctx")
    factor = 1.0 / math.sqrt(HEAD * rows * count_ctx)
    subs = rows // SUB
    inputs = (queries, key_vectors, value_vectors, out_grad)
    wide_spec = pl.BlockSpec((rows, PAIR), lambda p: (0, p))

    state, local = pl.pallas_call(
        lambda *refs: states_kernel(factor, *refs),
        grid=(pairs,),
        in_specs=[wide_spec] * 4,
        out_specs=(
            pl.BlockSpec((2, 2, HEAD, HEAD), lambda p: (0, p, 0, 0)),
            pl.BlockSpec((2, 2, subs - 1, HEAD, HEAD), lambda p: (0, p, 0, 0, 0)),
        ),
        out_shape=(
            jax.ShapeDtypeStruct((2, heads, HEAD, HEAD), BF16),
            jax.ShapeDtypeStruct((2, heads, subs - 1, HEAD, HEAD), BF16),
        ),
        cost_estimate=pl.CostEstimate(
            flops=4 * rows * width * HEAD, bytes_accessed=8 * rows * width, transcendentals=0
        ),
        name="states",
    )(*inputs)

    wide = jax.ShapeDtypeStruct((rows, width), BF16)
    partial = pl.pallas_call(
        lambda *refs: intra_kernel(factor, *refs),
        grid=(pairs,),
        in_specs=[wide_spec] * 4,
        out_specs=(wide_spec,) * 3,
        out_shape=(wide,) * 3,
        cost_estimate=pl.CostEstimate(
            flops=10 * rows * width * SUB, bytes_accessed=14 * rows * width, transcendentals=0
        ),
        name="intra",
    )(*inputs)

    index = lax.axis_index("ctx")
    core = index % 2
    chip = index // 2
    quarter = (chip ^ (chip >> 2)) & 1

    def swap(array, mask):
        return lax.ppermute(array, "ctx", [(i, i ^ mask) for i in range(count_ctx)])

    def mine_and_other(array, which):
        size = array.shape[1] // 2
        low, high = array[:, :size], array[:, size:]
        return jnp.where(which == 0, low, high), jnp.where(which == 0, high, low)

    def in_order(mine, other, which):
        return jnp.concatenate(
            [jnp.where(which == 0, mine, other), jnp.where(which == 0, other, mine)], 1
        )

    def add(a, b):
        return (a.astype(F32) + b.astype(F32)).astype(BF16)

    own_state, other_state = mine_and_other(state, core)
    core_state = swap(other_state, 1)
    chip_sum = add(own_state, core_state)
    own_sum, other_sum = mine_and_other(chip_sum, quarter)
    near_sum = swap(other_sum, 2)
    pair_sum = add(own_sum, near_sum)
    prefix = jnp.zeros(pair_sum.shape[1:], F32)
    suffix = prefix
    for step in (5, 2, 7):
        is_lower = chip < (chip ^ step)
        arrived = swap(jnp.where(is_lower, pair_sum[0], pair_sum[1]), 2 * step).astype(F32)
        prefix = prefix + jnp.where(is_lower, 0.0, arrived)
        suffix = suffix + jnp.where(is_lower, arrived, 0.0)
    is_first = (chip & 1) == 0
    near_wide = near_sum.astype(F32)
    own_wide = own_sum.astype(F32)
    for_near = jnp.stack(
        [
            prefix + jnp.where(is_first, own_wide[0], 0.0),
            suffix + jnp.where(is_first, 0.0, own_wide[1]),
        ]
    ).astype(BF16)
    from_near = swap(for_near, 2)
    mine = jnp.stack(
        [
            prefix + jnp.where(is_first, 0.0, near_wide[0]),
            suffix + jnp.where(is_first, near_wide[1], 0.0),
        ]
    ).astype(BF16)
    outer = in_order(mine, from_near, quarter)
    outer_wide = outer.astype(F32)
    state_wide = own_state.astype(F32)
    core_wide = core_state.astype(F32)
    for_core = jnp.stack(
        [
            outer_wide[0] + jnp.where(core == 0, state_wide[0], 0.0),
            outer_wide[1] + jnp.where(core == 0, 0.0, state_wide[1]),
        ]
    ).astype(BF16)
    from_core = swap(for_core, 1)
    mine = jnp.stack(
        [
            outer_wide[0] + jnp.where(core == 0, 0.0, core_wide[0]),
            outer_wide[1] + jnp.where(core == 0, core_wide[1], 0.0),
        ]
    ).astype(BF16)
    both = in_order(mine, from_core, core)

    return pl.pallas_call(
        final_kernel,
        grid=(pairs,),
        in_specs=[wide_spec] * 6
        + [
            pl.BlockSpec((None, 2, HEAD, HEAD), lambda p: (0, p, 0, 0)),
            pl.BlockSpec((None, 2, HEAD, HEAD), lambda p: (1, p, 0, 0)),
            pl.BlockSpec((2, 2, subs - 1, HEAD, HEAD), lambda p: (0, p, 0, 0, 0)),
        ],
        out_specs=(wide_spec,) * 3,
        out_shape=(wide,) * 3,
        cost_estimate=pl.CostEstimate(
            flops=6 * rows * width * HEAD, bytes_accessed=18 * rows * width, transcendentals=0
        ),
        name="final",
    )(key_vectors, value_vectors, out_grad, *partial, both, both, local)


def solution(mesh):
    spec = P(("dp", "ctx"), "tp")
    return jax.shard_map(
        on_device,
        mesh=mesh,
        in_specs=(spec,) * 4,
        out_specs=(spec,) * 3,
        check_vma=False,
    )
```

```python
import math

import jax
import jax.numpy as jnp
from jax import lax
from jax.experimental import pallas as pl
from jax.experimental.pallas import tpu as pltpu
from jax.sharding import PartitionSpec as P

HEAD = 128
SUB = 256
PAIR = 2 * HEAD
F32 = jnp.float32
BF16 = jnp.bfloat16
VMEM = pltpu.VMEM
MIB = 1 << 20

NN = (((1,), (0,)), ((), ()))
NT = (((1,), (1,)), ((), ()))
TN = (((0,), (0,)), ((), ()))


def places():
    index = lax.axis_index("ctx")
    core = lax.rem(index, 2)
    chip = lax.div(index, 2)
    low = lax.rem(chip, 2)
    quarter = lax.rem(low + lax.div(chip, 4), 2)
    return core, chip, low, quarter


def pair_columns(core, quarter, pair):
    of_core = core if pair < 2 else 1 - core
    of_quarter = quarter if pair % 2 == 0 else 1 - quarter
    return pl.ds(pl.multiple_of((2 * of_core + of_quarter) * PAIR, PAIR), PAIR)


def mm(a, b, dims):
    return lax.dot_general(a, b, dims, preferred_element_type=F32)


def call(kernel, name, args, outs, scratch=(), flops=0, traffic=0, limit=16, aliases=None):
    def placed(array, space):
        return array if space is pl.ANY else pltpu.with_memory_space_constraint(array, space)

    out_specs = tuple(
        pl.BlockSpec(memory_space=VMEM if space is VMEM else pltpu.HBM) for space, _ in outs
    )
    out_shape = tuple(
        VMEM(shape, BF16) if space is VMEM else jax.ShapeDtypeStruct(shape, BF16)
        for space, shape in outs
    )
    return pl.pallas_call(
        kernel,
        in_specs=[pl.BlockSpec(memory_space=space) for _, space in args],
        out_specs=out_specs,
        out_shape=out_shape,
        scratch_shapes=list(scratch),
        input_output_aliases=aliases or {},
        compiler_params=pltpu.CompilerParams(vmem_limit_bytes=limit * MIB),
        cost_estimate=pl.CostEstimate(flops=flops, bytes_accessed=traffic, transcendentals=0),
        name=name,
    )(*(placed(array, space) for array, space in args))


def states_kernel(first_pair, factor, *refs):
    sources = refs[:4]
    state_ref, local_ref = refs[-7:-5]
    held = refs[-5:-1]
    sems = refs[-1]
    core, _, _, quarter = places()

    def copy(pair, which):
        return pltpu.make_async_copy(
            sources[which].at[:, pair_columns(core, quarter, first_pair + pair)],
            held[which].at[pair],
            sems.at[pair, which],
        )

    order = (1, 2, 0, 3)
    for pair in range(2):
        for which in order:
            copy(pair, which).start()
    subs = held[0].shape[1] // SUB
    for pair in range(2):
        for kind, (left, right) in enumerate(((1, 2), (0, 3))):
            copy(pair, left).wait()
            copy(pair, right).wait()
            for head in range(2):
                cols = slice(head * HEAD, (head + 1) * HEAD)
                parts = []
                for sub in range(subs):
                    rows = slice(sub * SUB, (sub + 1) * SUB)
                    parts.append(
                        factor * mm(held[left][pair, rows, cols], held[right][pair, rows, cols], TN)
                    )
                if kind == 1:
                    parts = parts[::-1]
                total = parts[0]
                for sub in range(1, subs):
                    local_ref[kind, 2 * pair + head, sub - 1] = total.astype(BF16)
                    total = total + parts[sub]
                state_ref[kind, 2 * pair + head] = total.astype(BF16)


def intra_kernel(factor, q_ref, k_ref, v_ref, g_ref, _, gq_ref, gk_ref, gv_ref):
    row = lax.broadcasted_iota(jnp.int32, (SUB, SUB), 0)
    col = lax.broadcasted_iota(jnp.int32, (SUB, SUB), 1)
    subs = q_ref.shape[1] // SUB
    for pair in range(2):
        for head in range(2):
            cols = slice(head * HEAD, (head + 1) * HEAD)
            for sub in range(subs):
                rows = slice(sub * SUB, (sub + 1) * SUB)
                q, k, v, g = (ref[pair, rows, cols] for ref in (q_ref, k_ref, v_ref, g_ref))
                weights_t = jnp.where(col >= row, factor * mm(k, q, NT), 0.0).astype(BF16)
                upstream = jnp.where(row >= col, factor * mm(g, v, NT), 0.0).astype(BF16)
                gq_ref[pair, rows, cols] = mm(upstream, k, NN).astype(BF16)
                gk_ref[pair, rows, cols] = mm(upstream, q, TN).astype(BF16)
                gv_ref[pair, rows, cols] = mm(weights_t, g, NN).astype(BF16)


def pair_sum_kernel(own_ref, near_ref, _a, _b, _c, for_5, for_2, for_7):
    _, chip, _, _ = places()
    bit0, bit1, bit2 = lax.rem(chip, 2), lax.rem(lax.div(chip, 2), 2), lax.div(chip, 4)
    del bit0
    state = (own_ref[0].astype(F32) + near_ref[0].astype(F32)).astype(BF16)
    grad = (own_ref[1].astype(F32) + near_ref[1].astype(F32)).astype(BF16)
    for_5[...] = jnp.where(bit2 == 0, state, grad)
    for_2[...] = jnp.where(bit1 == 0, state, grad)
    for_7[...] = jnp.where(bit2 == 0, state, grad)


def add_where(base, condition, term):
    return base + jnp.where(condition, term.astype(F32), 0.0)


def pair_scan_kernel(
    from_5, from_2, from_7, own_sum, near_sum, own_state, core_state, _a, _b, _c, outer_ref, near_ref, wide_ref
):
    core, chip, low, _ = places()
    bit1, bit2 = lax.rem(lax.div(chip, 2), 2), lax.div(chip, 4)
    prefix = jnp.zeros(from_5.shape, F32)
    suffix = prefix
    for arrived, bit in ((from_5, bit2), (from_2, bit1), (from_7, bit2)):
        prefix = add_where(prefix, bit == 1, arrived[...])
        suffix = add_where(suffix, bit == 0, arrived[...])
    near_ref[0] = add_where(prefix, low == 0, own_sum[0]).astype(BF16)
    near_ref[1] = add_where(suffix, low == 1, own_sum[1]).astype(BF16)
    prefix = add_where(prefix, low == 1, near_sum[0])
    suffix = add_where(suffix, low == 0, near_sum[1])
    outer_ref[0] = add_where(prefix, core == 0, own_state[0, 0:2]).astype(BF16)
    outer_ref[1] = add_where(suffix, core == 1, own_state[1, 0:2]).astype(BF16)
    wide_ref[0] = add_where(prefix, core == 1, core_state[0, 0:2]).astype(BF16)
    wide_ref[1] = add_where(suffix, core == 0, core_state[1, 0:2]).astype(BF16)


def near_scan_kernel(from_near, outer, own_state, core_state, _, for_core_ref, wide_ref):
    core, _, _, _ = places()
    prefix = from_near[0].astype(F32)
    suffix = from_near[1].astype(F32)
    for_core_ref[:, 0:2] = outer[...]
    for_core_ref[0, 2:4] = add_where(prefix, core == 0, own_state[0, 2:4]).astype(BF16)
    for_core_ref[1, 2:4] = add_where(suffix, core == 1, own_state[1, 2:4]).astype(BF16)
    wide_ref[0] = add_where(prefix, core == 1, core_state[0, 2:4]).astype(BF16)
    wide_ref[1] = add_where(suffix, core == 0, core_state[1, 2:4]).astype(BF16)


def block_diagonal(first, second):
    zero = jnp.zeros_like(first)
    return jnp.concatenate(
        [jnp.concatenate([first, zero], 1), jnp.concatenate([zero, second], 1)], 0
    )


def final_kernel(first_pair, count, *refs):
    k_ref, v_ref, g_ref, gq_in, gk_in, gv_in, wide_ref, local_ref = refs[:8]
    outs = refs[-8:-5]
    token = refs[-5]
    buffers = refs[-4:-1]
    sems = refs[-1]
    core, _, _, quarter = places()
    subs = k_ref.shape[1] // SUB
    token[...] = jnp.zeros(token.shape, token.dtype)
    copies = []
    for step in range(count):
        pair = first_pair % 2 + step

        def of_sub(kind, terms):
            heads = []
            for head in range(2):
                wide = wide_ref[kind, 2 * step + head]
                if terms > 0:
                    wide = (
                        wide.astype(F32) + local_ref[kind, 2 * pair + head, terms - 1].astype(F32)
                    ).astype(BF16)
                heads.append(wide)
            return block_diagonal(*heads)

        for sub in range(subs):
            rows = slice(sub * SUB, (sub + 1) * SUB)
            prefix = of_sub(0, sub)
            suffix = of_sub(1, subs - 1 - sub)
            for buffer, base, rows_in, weight, dims in (
                (buffers[0], gq_in, g_ref, prefix, NT),
                (buffers[1], gk_in, v_ref, suffix, NT),
                (buffers[2], gv_in, k_ref, suffix, NN),
            ):
                buffer[step, rows, :] = (
                    base[pair, rows, :].astype(F32) + mm(rows_in[pair, rows, :], weight, dims)
                ).astype(BF16)
        for which in range(3):
            copy = pltpu.make_async_copy(
                buffers[which].at[step],
                outs[which].at[:, pair_columns(core, quarter, first_pair + step)],
                sems.at[step, which],
            )
            copy.start()
            copies.append(copy)
    for copy in copies:
        copy.wait()


def on_device(*inputs):
    rows, width = inputs[0].shape
    count_ctx = lax.axis_size("ctx")
    factor = 1.0 / math.sqrt(HEAD * rows * count_ctx)
    subs = rows // SUB
    held = (2, rows, PAIR)
    square = (HEAD, HEAD)

    def swap(array, mask):
        return lax.ppermute(array, "ctx", [(i, i ^ mask) for i in range(count_ctx)])

    def states(first_pair, name, *after):
        out = call(
            lambda *refs: states_kernel(first_pair, factor, *refs),
            name,
            [(array, pltpu.HBM) for array in inputs] + [(array, pl.ANY) for array in after],
            [(VMEM, (2, 4) + square), (VMEM, (2, 4, subs - 1) + square)] + [(VMEM, held)] * 4,
            scratch=[pltpu.SemaphoreType.DMA((2, 4))],
            flops=2 * rows * width * HEAD,
            traffic=4 * rows * width,
        )
        return out[0], out[1], out[2:]

    def intra(arrays, name, after):
        return call(
            lambda *refs: intra_kernel(factor, *refs),
            name,
            [(array, VMEM) for array in arrays] + [(after, pl.ANY)],
            [(VMEM, held)] * 3,
            flops=5 * rows * width * SUB,
            traffic=7 * rows * width,
        )

    def final(first_pair, count, name, arrays, partial, wide, local, outs):
        before = [(array, pltpu.HBM) for array in outs]
        return call(
            lambda *refs: final_kernel(first_pair, count, *refs),
            name,
            [(array, VMEM) for array in (*arrays[1:], *partial, wide, local)] + before,
            [(pltpu.HBM, (rows, width))] * 3 + [(VMEM, (16, HEAD))],
            scratch=[pltpu.VMEM((count, rows, PAIR), BF16)] * 3 + [pltpu.SemaphoreType.DMA((count, 3))],
            flops=3 * rows * PAIR * PAIR * count,
            traffic=6 * rows * PAIR * count,
            aliases={8 + i: i for i in range(len(before))},
        )

    other_state, other_local, other_held = states(2, "states_other")
    core_state = swap(other_state, 1)
    own_state, own_local, own_held = states(0, "states_own", other_state)
    chip_sum = (own_state.astype(F32) + core_state.astype(F32)).astype(BF16)
    own_sum, other_sum = chip_sum[:, 0:2], chip_sum[:, 2:4]
    near_sum = swap(other_sum, 2)
    other_partial = intra(other_held, "intra_other", other_sum)

    sends = call(
        pair_sum_kernel,
        "pair_sum",
        [(own_sum, VMEM), (near_sum, VMEM)] + [(array, pl.ANY) for array in other_partial],
        [(VMEM, (2,) + square)] * 3,
    )
    arrived = [swap(array, 2 * mask) for array, mask in zip(sends, (5, 2, 7))]
    own_partial = intra(own_held, "intra_own", sends[0])
    outer, for_near, wide_0 = call(
        pair_scan_kernel,
        "pair_scan",
        [(array, VMEM) for array in (*arrived, own_sum, near_sum, own_state, core_state)]
        + [(array, pl.ANY) for array in own_partial],
        [(VMEM, (2, 2) + square)] * 3,
    )
    from_near = swap(for_near, 2)
    *outs, token = final(0, 1, "final_0", own_held, own_partial, wide_0, own_local, ())
    for_core, wide_1 = call(
        near_scan_kernel,
        "near_scan",
        [(array, VMEM) for array in (from_near, outer, own_state, core_state)] + [(token, pl.ANY)],
        [(VMEM, (2, 4) + square), (VMEM, (2, 2) + square)],
    )
    from_core = swap(for_core, 1)
    *outs, token = final(1, 1, "final_1", own_held, own_partial, wide_1, own_local, outs)
    *outs, token = final(2, 2, "final_2", other_held, other_partial, from_core, other_local, outs)
    return tuple(outs)


def solution(mesh):
    spec = P(("dp", "ctx"), "tp")
    return jax.shard_map(
        on_device,
        mesh=mesh,
        in_specs=(spec,) * 4,
        out_specs=(spec,) * 3,
        check_vma=False,
    )
```

```python
import math

import jax
import jax.numpy as jnp
from jax import lax
from jax.experimental import pallas as pl
from jax.experimental.pallas import tpu as pltpu
from jax.sharding import PartitionSpec as P

HEAD = 128
SUB = 256
PAIR = 2 * HEAD
F32 = jnp.float32
BF16 = jnp.bfloat16
VMEM = pltpu.VMEM
MIB = 1 << 20
STEPS = (2, 5, 7)

NN = (((1,), (0,)), ((), ()))
NT = (((1,), (1,)), ((), ()))
TN = (((0,), (0,)), ((), ()))


def places():
    index = lax.axis_index("ctx")
    core = lax.rem(index, 2)
    chip = lax.div(index, 2)
    low = lax.rem(chip, 2)
    quarter = lax.rem(low + lax.div(chip, 4), 2)
    return core, chip, low, quarter


def pair_columns(core, quarter, pair):
    of_core = core if pair < 2 else 1 - core
    of_quarter = quarter if pair % 2 == 0 else 1 - quarter
    return pl.ds(pl.multiple_of((2 * of_core + of_quarter) * PAIR, PAIR), PAIR)


def mm(a, b, dims):
    return lax.dot_general(a, b, dims, preferred_element_type=F32)


def call(kernel, name, args, outs, scratch=(), limit=16, aliases=None):
    def placed(array, space):
        return array if space is pl.ANY else pltpu.with_memory_space_constraint(array, space)

    out_specs = tuple(
        pl.BlockSpec(memory_space=VMEM if space is VMEM else pltpu.HBM) for space, _ in outs
    )
    out_shape = tuple(
        VMEM(shape, BF16) if space is VMEM else jax.ShapeDtypeStruct(shape, BF16)
        for space, shape in outs
    )
    return pl.pallas_call(
        kernel,
        in_specs=[pl.BlockSpec(memory_space=space) for _, space in args],
        out_specs=out_specs,
        out_shape=out_shape,
        scratch_shapes=list(scratch),
        input_output_aliases=aliases or {},
        compiler_params=pltpu.CompilerParams(vmem_limit_bytes=limit * MIB),
        cost_estimate=pl.CostEstimate(flops=0, bytes_accessed=0, transcendentals=0),
        name=name,
    )(*(placed(array, space) for array, space in args))


def states_kernel(pairs, factor, *refs):
    sources = refs[:4]
    results = refs[-5 * len(pairs) - 2 : -1]
    state_ref = results[0]
    sems = refs[-1]
    core, _, _, quarter = places()
    subs = sources[0].shape[0] // SUB

    def copy(step, which):
        return pltpu.make_async_copy(
            sources[which].at[:, pair_columns(core, quarter, pairs[step])],
            results[5 * step + 2 + which],
            sems.at[step, which],
        )

    for step in range(len(pairs)):
        for which in (1, 2, 0, 3):
            copy(step, which).start()
    for step in range(len(pairs)):
        local_ref, *held = results[5 * step + 1 : 5 * step + 6]
        for kind, (left, right) in enumerate(((1, 2), (0, 3))):
            copy(step, left).wait()
            copy(step, right).wait()
            for head in range(2):
                cols = slice(head * HEAD, (head + 1) * HEAD)
                parts = []
                for sub in range(subs):
                    rows = slice(sub * SUB, (sub + 1) * SUB)
                    parts.append(factor * mm(held[left][rows, cols], held[right][rows, cols], TN))
                if kind == 1:
                    parts = parts[::-1]
                total = parts[0]
                for sub in range(1, subs):
                    local_ref[kind, head, sub - 1] = total.astype(BF16)
                    total = total + parts[sub]
                state_ref[step, kind, head] = total.astype(BF16)


def intra_kernel(factor, q_ref, k_ref, v_ref, g_ref, _, gq_ref, gk_ref, gv_ref):
    row = lax.broadcasted_iota(jnp.int32, (SUB, SUB), 0)
    col = lax.broadcasted_iota(jnp.int32, (SUB, SUB), 1)
    subs = q_ref.shape[0] // SUB
    for head in range(2):
        cols = slice(head * HEAD, (head + 1) * HEAD)
        for sub in range(subs):
            rows = slice(sub * SUB, (sub + 1) * SUB)
            q, k, v, g = (ref[rows, cols] for ref in (q_ref, k_ref, v_ref, g_ref))
            weights_t = jnp.where(col >= row, factor * mm(k, q, NT), 0.0).astype(BF16)
            upstream = jnp.where(row >= col, factor * mm(g, v, NT), 0.0).astype(BF16)
            gq_ref[rows, cols] = mm(upstream, k, NN).astype(BF16)
            gk_ref[rows, cols] = mm(upstream, q, TN).astype(BF16)
            gv_ref[rows, cols] = mm(weights_t, g, NN).astype(BF16)


def add_where(base, condition, term):
    return base + jnp.where(condition, term.astype(F32), 0.0)


def upper_bit(chip, step):
    return lax.rem(lax.div(chip, 1 << (step.bit_length() - 1)), 2)


def pair_sum_kernel(own_ref, core_ref, near_sum, *refs):
    own_state, core_state = own_ref.at[0], core_ref.at[1]
    outs = refs[-3:]
    _, chip, _, _ = places()
    state, grad = (
        (own_state[i].astype(F32) + core_state[i].astype(F32) + near_sum[i].astype(F32)).astype(BF16)
        for i in range(2)
    )
    for step, out in zip(STEPS, outs):
        out[...] = jnp.where(upper_bit(chip, step) == 0, state, grad)


def pair_scan_kernel(*refs):
    arrived = refs[:3]
    own_ref, core_ref, near_sum = refs[3:6]
    own_state, core_state = own_ref.at[0], core_ref.at[1]
    near_ref, outer_ref, wide_ref = refs[-3:]
    core, chip, low, _ = places()
    sums = [jnp.zeros(arrived[0].shape, F32)] * 2
    for step, term in zip(STEPS, arrived):
        bit = upper_bit(chip, step)
        sums = [add_where(sums[i], bit == 1 - i, term[...]) for i in range(2)]
    for i in range(2):
        own = own_state[i].astype(F32)
        other = core_state[i].astype(F32)
        near_ref[i] = add_where(sums[i], low == i, own + other).astype(BF16)
        total = add_where(sums[i], low == 1 - i, near_sum[i])
        outer_ref[i] = add_where(total, core == i, own).astype(BF16)
        wide_ref[i] = add_where(total, core == 1 - i, other).astype(BF16)


def near_scan_kernel(from_near, own_ref, core_ref, *refs):
    own_state, core_state = own_ref.at[0], core_ref.at[0]
    outer_ref, wide_ref = refs[-2:]
    core, _, _, _ = places()
    for i in range(2):
        total = from_near[i].astype(F32)
        outer_ref[i] = add_where(total, core == i, own_state[i]).astype(BF16)
        wide_ref[i] = add_where(total, core == 1 - i, core_state[i]).astype(BF16)


def block_diagonal(first, second):
    zero = jnp.zeros_like(first)
    return jnp.concatenate(
        [jnp.concatenate([first, zero], 1), jnp.concatenate([zero, second], 1)], 0
    )


def final_kernel(pairs, ready, keep, *refs):
    waiting = refs[8 * len(pairs) : 8 * len(pairs) + 3 * len(ready)]
    sems = refs[-1]
    core, _, _, quarter = places()
    copies = []
    count = 3 * len(pairs)
    if keep:
        *outs, token = refs[-2 - count - 3 * bool(ready) : -1 - count]
    else:
        *outs, token = refs[-2 - count - 3 : -1 - count]
    buffers = refs[-1 - count : -1]
    token[...] = jnp.zeros(token.shape, token.dtype)

    def send(buffer, pair, which, row, size):
        rows = pl.ds(row, size)
        copy = pltpu.make_async_copy(
            buffer.at[rows],
            outs[which].at[rows, pair_columns(core, quarter, pair)],
            sems.at[len(copies)],
        )
        copy.start()
        copies.append(copy)

    for step, pair in enumerate(ready):
        for which in range(3):
            buffer = waiting[3 * step + which]
            send(buffer, pair, which, 0, buffer.shape[0])
    for step, pair in enumerate(pairs):
        k_ref, v_ref, g_ref, gq_in, gk_in, gv_in, wide_ref, local_ref = refs[8 * step : 8 * step + 8]
        subs = k_ref.shape[0] // SUB

        def of_sub(kind, terms):
            heads = []
            for head in range(2):
                wide = wide_ref[kind, head]
                if terms > 0:
                    wide = (
                        wide.astype(F32) + local_ref[kind, head, terms - 1].astype(F32)
                    ).astype(BF16)
                heads.append(wide)
            return block_diagonal(*heads)

        for sub in range(subs):
            rows = slice(sub * SUB, (sub + 1) * SUB)
            prefix = of_sub(0, sub)
            suffix = of_sub(1, subs - 1 - sub)
            for which, (base, rows_in, weight, dims) in enumerate(
                ((gq_in, g_ref, prefix, NT), (gk_in, v_ref, suffix, NT), (gv_in, k_ref, suffix, NN))
            ):
                buffer = buffers[3 * step + which]
                buffer[rows, :] = (
                    base[rows, :].astype(F32) + mm(rows_in[rows, :], weight, dims)
                ).astype(BF16)
                if not keep:
                    send(buffer, pair, which, sub * SUB, SUB)
    for copy in copies:
        copy.wait()


def on_device(*inputs):
    rows, width = inputs[0].shape
    count_ctx = lax.axis_size("ctx")
    factor = 1.0 / math.sqrt(HEAD * rows * count_ctx)
    subs = rows // SUB
    held = (rows, PAIR)
    square = (HEAD, HEAD)

    def swap(array, mask):
        return lax.ppermute(array, "ctx", [(i, i ^ mask) for i in range(count_ctx)])

    def states(pairs, *after):
        state, *out = call(
            lambda *refs: states_kernel(pairs, factor, *refs),
            "states_" + "_".join(map(str, pairs)),
            [(array, pltpu.HBM) for array in inputs] + [(array, pl.ANY) for array in after],
            [(VMEM, (len(pairs), 2, 2) + square)]
            + ([(VMEM, (2, 2, subs - 1) + square)] + [(VMEM, held)] * 4) * len(pairs),
            scratch=[pltpu.SemaphoreType.DMA((len(pairs), 4))],
        )
        return state, *((out[i], out[i + 1 : i + 5]) for i in range(0, len(out), 5))

    def intra(pair, arrays, after):
        return call(
            lambda *refs: intra_kernel(factor, *refs),
            f"intra_{pair}",
            [(array, VMEM) for array in arrays] + [(after, pl.ANY)],
            [(VMEM, held)] * 3,
        )

    def scan(kernel, name, args, after, count):
        return call(
            kernel,
            name,
            [(array, VMEM) for array in args] + [(array, pl.ANY) for array in after],
            count,
        )

    def final(parts, outs, ready=None, keep=False):
        ready = ready or {}
        args = []
        for arrays, partial, wide, local in parts.values():
            args += [(array, VMEM) for array in (*arrays[1:], *partial, wide, local)]
        for arrays in ready.values():
            args += [(array, VMEM) for array in arrays]
        count = len(parts)
        sends = 3 * len(ready) + (0 if keep else 3 * subs * count)
        to_outs = [(pltpu.HBM, (rows, width))] * (3 if sends else 0)
        results = [(VMEM, held)] * 3 * count
        out = call(
            lambda *refs: final_kernel(tuple(parts), tuple(ready), keep, *refs),
            "final_" + "_".join(map(str, parts)),
            args + [(array, pltpu.HBM) for array in outs],
            to_outs + [(VMEM, (16, HEAD))] + (results if keep else []),
            scratch=([] if keep else [pltpu.VMEM(held, BF16)] * 3 * count)
            + [pltpu.SemaphoreType.DMA((max(sends, 1),))],
            aliases={len(args) + i: i for i in range(len(outs))},
        )
        return out[: len(to_outs)], out[len(to_outs)], out[len(to_outs) + 1 :]

    quarter = (2, 2) + square
    state_32, (local_3, held_3), (local_2, held_2) = states((3, 2))
    core_10 = swap(state_32, 1)
    state_1, (local_1, held_1) = states((1,), state_32)
    sum_1 = (state_1[0].astype(F32) + core_10[0].astype(F32)).astype(BF16)
    near_0 = swap(sum_1, 2)
    state_0, (local_0, held_0) = states((0,), sum_1)
    partial_3 = intra(3, held_3, sum_1)
    sends = scan(
        pair_sum_kernel, "pair_sum", (state_0, core_10, near_0), partial_3, [(VMEM, (2,) + square)] * 3
    )
    arrived = [swap(array, 2 * step) for step, array in zip(STEPS, sends)]
    partial_1 = intra(1, held_1, sends[0])
    partial_0 = intra(0, held_0, sends[0])
    for_near, outer_0, wide_0 = scan(
        pair_scan_kernel,
        "pair_scan",
        (*arrived, state_0, core_10, near_0),
        (*partial_1, *partial_0),
        [(VMEM, quarter)] * 3,
    )
    from_near = swap(for_near, 2)
    wide_2 = swap(outer_0, 1)
    partial_2 = intra(2, held_2, for_near)
    outs, token, _ = final(
        {0: (held_0, partial_0, wide_0, local_0), 2: (held_2, partial_2, wide_2, local_2)}, ()
    )
    outer_1, wide_1 = scan(
        near_scan_kernel,
        "near_scan",
        (from_near, state_1, core_10),
        (token,),
        [(VMEM, quarter)] * 2,
    )
    wide_3 = swap(outer_1, 1)
    _, _, ready_1 = final({1: (held_1, partial_1, wide_1, local_1)}, (), keep=True)
    outs, _, _ = final({3: (held_3, partial_3, wide_3, local_3)}, outs, ready={1: ready_1})
    return tuple(outs)


def solution(mesh):
    spec = P(("dp", "ctx"), "tp")
    return jax.shard_map(
        on_device,
        mesh=mesh,
        in_specs=(spec,) * 4,
        out_specs=(spec,) * 3,
        check_vma=False,
    )
```

```python
import math

import jax
import jax.numpy as jnp
from jax import lax
from jax.experimental import pallas as pl
from jax.experimental.pallas import tpu as pltpu
from jax.sharding import PartitionSpec as P

HEAD = 128
SUB = 256
PAIR = 2 * HEAD
F32 = jnp.float32
BF16 = jnp.bfloat16
VMEM = pltpu.VMEM
MIB = 1 << 20
STEPS = (5,7,2)

NN = (((1,), (0,)), ((), ()))
NT = (((1,), (1,)), ((), ()))
TN = (((0,), (0,)), ((), ()))


def places():
    index = lax.axis_index("ctx")
    core = lax.rem(index, 2)
    chip = lax.div(index, 2)
    low = lax.rem(chip, 2)
    quarter = lax.rem(low + lax.div(chip, 4), 2)
    return core, chip, low, quarter


def pair_columns(core, quarter, pair):
    of_core = core if pair < 2 else 1 - core
    of_quarter = quarter if pair % 2 == 0 else 1 - quarter
    return pl.ds(pl.multiple_of((2 * of_core + of_quarter) * PAIR, PAIR), PAIR)


def mm(a, b, dims):
    return lax.dot_general(a, b, dims, preferred_element_type=F32)


def call(kernel, name, args, outs, scratch=(), limit=16, aliases=None):
    def placed(array, space):
        return array if space is pl.ANY else pltpu.with_memory_space_constraint(array, space)

    out_specs = tuple(
        pl.BlockSpec(memory_space=VMEM if space is VMEM else pltpu.HBM) for space, _ in outs
    )
    out_shape = tuple(
        VMEM(shape, BF16) if space is VMEM else jax.ShapeDtypeStruct(shape, BF16)
        for space, shape in outs
    )
    return pl.pallas_call(
        kernel,
        in_specs=[pl.BlockSpec(memory_space=space) for _, space in args],
        out_specs=out_specs,
        out_shape=out_shape,
        scratch_shapes=list(scratch),
        input_output_aliases=aliases or {},
        compiler_params=pltpu.CompilerParams(vmem_limit_bytes=limit * MIB),
        cost_estimate=pl.CostEstimate(flops=0, bytes_accessed=0, transcendentals=0),
        name=name,
    )(*(placed(array, space) for array, space in args))


def states_kernel(pairs, factor, *refs):
    sources = refs[:4]
    results = refs[-5 * len(pairs) - 2 : -1]
    state_ref = results[0]
    sems = refs[-1]
    core, _, _, quarter = places()
    subs = sources[0].shape[0] // SUB

    def copy(step, which):
        return pltpu.make_async_copy(
            sources[which].at[:, pair_columns(core, quarter, pairs[step])],
            results[5 * step + 2 + which],
            sems.at[step, which],
        )

    for step in range(len(pairs)):
        for which in (1, 2, 0, 3):
            copy(step, which).start()
    for step in range(len(pairs)):
        local_ref, *held = results[5 * step + 1 : 5 * step + 6]
        for kind, (left, right) in enumerate(((1, 2), (0, 3))):
            copy(step, left).wait()
            copy(step, right).wait()
            for head in range(2):
                cols = slice(head * HEAD, (head + 1) * HEAD)
                parts = []
                for sub in range(subs):
                    rows = slice(sub * SUB, (sub + 1) * SUB)
                    parts.append(factor * mm(held[left][rows, cols], held[right][rows, cols], TN))
                if kind == 1:
                    parts = parts[::-1]
                total = parts[0]
                for sub in range(1, subs):
                    local_ref[kind, head, sub - 1] = total.astype(BF16)
                    total = total + parts[sub]
                state_ref[step, kind, head] = total.astype(BF16)


def intra_kernel(factor, q_ref, k_ref, v_ref, g_ref, _, gq_ref, gk_ref, gv_ref):
    row = lax.broadcasted_iota(jnp.int32, (SUB, SUB), 0)
    col = lax.broadcasted_iota(jnp.int32, (SUB, SUB), 1)
    subs = q_ref.shape[0] // SUB
    for head in range(2):
        cols = slice(head * HEAD, (head + 1) * HEAD)
        for sub in range(subs):
            rows = slice(sub * SUB, (sub + 1) * SUB)
            q, k, v, g = (ref[rows, cols] for ref in (q_ref, k_ref, v_ref, g_ref))
            weights_t = jnp.where(col >= row, factor * mm(k, q, NT), 0.0).astype(BF16)
            upstream = jnp.where(row >= col, factor * mm(g, v, NT), 0.0).astype(BF16)
            gq_ref[rows, cols] = mm(upstream, k, NN).astype(BF16)
            gk_ref[rows, cols] = mm(upstream, q, TN).astype(BF16)
            gv_ref[rows, cols] = mm(weights_t, g, NN).astype(BF16)


def add_where(base, condition, term):
    return base + jnp.where(condition, term.astype(F32), 0.0)


def upper_bit(chip, step):
    return lax.rem(lax.div(chip, 1 << (step.bit_length() - 1)), 2)


def pair_sum_kernel(own_ref, core_ref, near_sum, *refs):
    own_state, core_state = own_ref.at[0], core_ref.at[1]
    outs = refs[-3:]
    _, chip, _, _ = places()
    state, grad = (
        (own_state[i].astype(F32) + core_state[i].astype(F32) + near_sum[i].astype(F32)).astype(BF16)
        for i in range(2)
    )
    for step, out in zip(STEPS, outs):
        out[...] = jnp.where(upper_bit(chip, step) == 0, state, grad)


def pair_scan_kernel(*refs):
    arrived = refs[:3]
    own_ref, core_ref, near_sum = refs[3:6]
    own_state, core_state = own_ref.at[0], core_ref.at[1]
    near_ref, outer_ref, wide_ref = refs[-3:]
    core, chip, low, _ = places()
    sums = [jnp.zeros(arrived[0].shape, F32)] * 2
    for step, term in zip(STEPS, arrived):
        bit = upper_bit(chip, step)
        sums = [add_where(sums[i], bit == 1 - i, term[...]) for i in range(2)]
    for i in range(2):
        own = own_state[i].astype(F32)
        other = core_state[i].astype(F32)
        near_ref[i] = add_where(sums[i], low == i, own + other).astype(BF16)
        total = add_where(sums[i], low == 1 - i, near_sum[i])
        outer_ref[i] = add_where(total, core == i, own).astype(BF16)
        wide_ref[i] = add_where(total, core == 1 - i, other).astype(BF16)


def near_scan_kernel(from_near, own_ref, core_ref, *refs):
    own_state, core_state = own_ref.at[0], core_ref.at[0]
    outer_ref, wide_ref = refs[-2:]
    core, _, _, _ = places()
    for i in range(2):
        total = from_near[i].astype(F32)
        outer_ref[i] = add_where(total, core == i, own_state[i]).astype(BF16)
        wide_ref[i] = add_where(total, core == 1 - i, core_state[i]).astype(BF16)


def block_diagonal(first, second):
    zero = jnp.zeros_like(first)
    return jnp.concatenate(
        [jnp.concatenate([first, zero], 1), jnp.concatenate([zero, second], 1)], 0
    )


def final_kernel(pairs, ready, keep, *refs):
    waiting = refs[8 * len(pairs) : 8 * len(pairs) + 3 * len(ready)]
    sems = refs[-1]
    core, _, _, quarter = places()
    copies = []
    count = 3 * len(pairs)
    if keep:
        *outs, token = refs[-2 - count - 3 * bool(ready) : -1 - count]
    else:
        *outs, token = refs[-2 - count - 3 : -1 - count]
    buffers = refs[-1 - count : -1]
    token[...] = jnp.zeros(token.shape, token.dtype)

    def send(buffer, pair, which, row, size):
        rows = pl.ds(row, size)
        copy = pltpu.make_async_copy(
            buffer.at[rows],
            outs[which].at[rows, pair_columns(core, quarter, pair)],
            sems.at[len(copies)],
        )
        copy.start()
        copies.append(copy)

    for step, pair in enumerate(ready):
        for which in range(3):
            buffer = waiting[3 * step + which]
            send(buffer, pair, which, 0, buffer.shape[0])
    for step, pair in enumerate(pairs):
        k_ref, v_ref, g_ref, gq_in, gk_in, gv_in, wide_ref, local_ref = refs[8 * step : 8 * step + 8]
        subs = k_ref.shape[0] // SUB

        def of_sub(kind, terms):
            heads = []
            for head in range(2):
                wide = wide_ref[kind, head]
                if terms > 0:
                    wide = (
                        wide.astype(F32) + local_ref[kind, head, terms - 1].astype(F32)
                    ).astype(BF16)
                heads.append(wide)
            return block_diagonal(*heads)

        for sub in range(subs):
            rows = slice(sub * SUB, (sub + 1) * SUB)
            prefix = of_sub(0, sub)
            suffix = of_sub(1, subs - 1 - sub)
            for which, (base, rows_in, weight, dims) in enumerate(
                ((gq_in, g_ref, prefix, NT), (gk_in, v_ref, suffix, NT), (gv_in, k_ref, suffix, NN))
            ):
                buffer = buffers[3 * step + which]
                buffer[rows, :] = (
                    base[rows, :].astype(F32) + mm(rows_in[rows, :], weight, dims)
                ).astype(BF16)
                if not keep:
                    send(buffer, pair, which, sub * SUB, SUB)
    for copy in copies:
        copy.wait()


def on_device(*inputs):
    rows, width = inputs[0].shape
    count_ctx = lax.axis_size("ctx")
    factor = 1.0 / math.sqrt(HEAD * rows * count_ctx)
    subs = rows // SUB
    held = (rows, PAIR)
    square = (HEAD, HEAD)

    def swap(array, mask):
        return lax.ppermute(array, "ctx", [(i, i ^ mask) for i in range(count_ctx)])

    def states(pairs, *after):
        state, *out = call(
            lambda *refs: states_kernel(pairs, factor, *refs),
            "states_" + "_".join(map(str, pairs)),
            [(array, pltpu.HBM) for array in inputs] + [(array, pl.ANY) for array in after],
            [(VMEM, (len(pairs), 2, 2) + square)]
            + ([(VMEM, (2, 2, subs - 1) + square)] + [(VMEM, held)] * 4) * len(pairs),
            scratch=[pltpu.SemaphoreType.DMA((len(pairs), 4))],
        )
        return state, *((out[i], out[i + 1 : i + 5]) for i in range(0, len(out), 5))

    def intra(pair, arrays, after):
        return call(
            lambda *refs: intra_kernel(factor, *refs),
            f"intra_{pair}",
            [(array, VMEM) for array in arrays] + [(after, pl.ANY)],
            [(VMEM, held)] * 3,
        )

    def scan(kernel, name, args, after, count):
        return call(
            kernel,
            name,
            [(array, VMEM) for array in args] + [(array, pl.ANY) for array in after],
            count,
        )

    def final(parts, outs, ready=None, keep=False):
        ready = ready or {}
        args = []
        for arrays, partial, wide, local in parts.values():
            args += [(array, VMEM) for array in (*arrays[1:], *partial, wide, local)]
        for arrays in ready.values():
            args += [(array, VMEM) for array in arrays]
        count = len(parts)
        sends = 3 * len(ready) + (0 if keep else 3 * subs * count)
        to_outs = [(pltpu.HBM, (rows, width))] * (3 if sends else 0)
        results = [(VMEM, held)] * 3 * count
        out = call(
            lambda *refs: final_kernel(tuple(parts), tuple(ready), keep, *refs),
            "final_" + "_".join(map(str, parts)),
            args + [(array, pltpu.HBM) for array in outs],
            to_outs + [(VMEM, (16, HEAD))] + (results if keep else []),
            scratch=([] if keep else [pltpu.VMEM(held, BF16)] * 3 * count)
            + [pltpu.SemaphoreType.DMA((max(sends, 1),))],
            aliases={len(args) + i: i for i in range(len(outs))},
        )
        return out[: len(to_outs)], out[len(to_outs)], out[len(to_outs) + 1 :]

    quarter = (2, 2) + square
    state_32, (local_3, held_3), (local_2, held_2) = states((3, 2))
    core_10 = swap(state_32, 1)
    state_1, (local_1, held_1) = states((1,), state_32)
    sum_1 = (state_1[0].astype(F32) + core_10[0].astype(F32)).astype(BF16)
    near_0 = swap(sum_1, 2)
    state_0, (local_0, held_0) = states((0,), sum_1)
    partial_3 = intra(3, held_3, sum_1)
    sends = scan(
        pair_sum_kernel, "pair_sum", (state_0, core_10, near_0), partial_3, [(VMEM, (2,) + square)] * 3
    )
    arrived = [swap(array, 2 * step) for step, array in zip(STEPS, sends)]
    partial_1 = intra(1, held_1, sends[0])
    partial_0 = intra(0, held_0, sends[0])
    for_near, outer_0, wide_0 = scan(
        pair_scan_kernel,
        "pair_scan",
        (*arrived, state_0, core_10, near_0),
        (*partial_1, *partial_0),
        [(VMEM, quarter)] * 3,
    )
    from_near = swap(for_near, 2)
    wide_2 = swap(outer_0, 1)
    partial_2 = intra(2, held_2, for_near)
    outs, token, _ = final({0: (held_0, partial_0, wide_0, local_0)}, ())
    outer_1, wide_1 = scan(
        near_scan_kernel,
        "near_scan",
        (from_near, state_1, core_10),
        (token, *partial_2),
        [(VMEM, quarter)] * 2,
    )
    wide_3 = swap(outer_1, 1)
    _, _, kept = final(
        {1: (held_1, partial_1, wide_1, local_1), 2: (held_2, partial_2, wide_2, local_2)},
        (),
        keep=True,
    )
    outs, _, _ = final(
        {3: (held_3, partial_3, wide_3, local_3)}, outs, ready={1: kept[:3], 2: kept[3:]}
    )
    return tuple(outs)


def solution(mesh):
    spec = P(("dp", "ctx"), "tp")
    return jax.shard_map(
        on_device,
        mesh=mesh,
        in_specs=(spec,) * 4,
        out_specs=(spec,) * 3,
        check_vma=False,
    )
```

```python
import math

import jax
import jax.numpy as jnp
from jax import lax
from jax.experimental import pallas as pl
from jax.experimental.pallas import tpu as pltpu
from jax.sharding import PartitionSpec as P

HEAD = 128
SUB = 256
PAIR = 2 * HEAD
F32 = jnp.float32
BF16 = jnp.bfloat16
VMEM = pltpu.VMEM
MIB = 1 << 20
STEPS = (5,7,2)

NN = (((1,), (0,)), ((), ()))
NT = (((1,), (1,)), ((), ()))
TN = (((0,), (0,)), ((), ()))


def places():
    index = lax.axis_index("ctx")
    core = lax.rem(index, 2)
    chip = lax.div(index, 2)
    low = lax.rem(chip, 2)
    quarter = lax.rem(low + lax.div(chip, 4), 2)
    return core, chip, low, quarter


def pair_columns(half, quarter, pair):
    of_core = half if pair < 2 else 1 - half
    of_quarter = quarter if pair % 2 == 0 else 1 - quarter
    return pl.ds(pl.multiple_of((2 * of_core + of_quarter) * PAIR, PAIR), PAIR)


def mm(a, b, dims):
    return lax.dot_general(a, b, dims, preferred_element_type=F32)


def call(kernel, name, args, outs, scratch=(), limit=16, aliases=None):
    def placed(array, space):
        return array if space is pl.ANY else pltpu.with_memory_space_constraint(array, space)

    out_specs = tuple(
        pl.BlockSpec(memory_space=VMEM if space is VMEM else pltpu.HBM) for space, _ in outs
    )
    out_shape = tuple(
        VMEM(shape, BF16) if space is VMEM else jax.ShapeDtypeStruct(shape, BF16)
        for space, shape in outs
    )
    return pl.pallas_call(
        kernel,
        in_specs=[pl.BlockSpec(memory_space=space) for _, space in args],
        out_specs=out_specs,
        out_shape=out_shape,
        scratch_shapes=list(scratch),
        input_output_aliases=aliases or {},
        compiler_params=pltpu.CompilerParams(vmem_limit_bytes=limit * MIB),
        cost_estimate=pl.CostEstimate(flops=0, bytes_accessed=0, transcendentals=0),
        name=name,
    )(*(placed(array, space) for array, space in args))


def states_kernel(pairs, factor, *refs):
    sources = refs[:4]
    results = refs[-5 * len(pairs) - 2 : -1]
    state_ref = results[0]
    sems = refs[-1]
    core, _, low, quarter = places()
    half = lax.rem(core + low, 2)
    subs = sources[0].shape[0] // SUB

    def copy(step, which):
        return pltpu.make_async_copy(
            sources[which].at[:, pair_columns(half, quarter, pairs[step])],
            results[5 * step + 2 + which],
            sems.at[step, which],
        )

    for step in range(len(pairs)):
        for which in (1, 2, 0, 3):
            copy(step, which).start()
    for step in range(len(pairs)):
        local_ref, *held = results[5 * step + 1 : 5 * step + 6]
        for kind, (left, right) in enumerate(((1, 2), (0, 3))):
            copy(step, left).wait()
            copy(step, right).wait()
            for head in range(2):
                cols = slice(head * HEAD, (head + 1) * HEAD)
                parts = []
                for sub in range(subs):
                    rows = slice(sub * SUB, (sub + 1) * SUB)
                    parts.append(factor * mm(held[left][rows, cols], held[right][rows, cols], TN))
                if kind == 1:
                    parts = parts[::-1]
                total = parts[0]
                for sub in range(1, subs):
                    local_ref[kind, head, sub - 1] = total.astype(BF16)
                    total = total + parts[sub]
                state_ref[step, kind, head] = total.astype(BF16)


def intra_kernel(factor, q_ref, k_ref, v_ref, g_ref, _, gq_ref, gk_ref, gv_ref):
    row = lax.broadcasted_iota(jnp.int32, (SUB, SUB), 0)
    col = lax.broadcasted_iota(jnp.int32, (SUB, SUB), 1)
    subs = q_ref.shape[0] // SUB
    for head in range(2):
        cols = slice(head * HEAD, (head + 1) * HEAD)
        for sub in range(subs):
            rows = slice(sub * SUB, (sub + 1) * SUB)
            q, k, v, g = (ref[rows, cols] for ref in (q_ref, k_ref, v_ref, g_ref))
            weights_t = jnp.where(col >= row, factor * mm(k, q, NT), 0.0).astype(BF16)
            upstream = jnp.where(row >= col, factor * mm(g, v, NT), 0.0).astype(BF16)
            gq_ref[rows, cols] = mm(upstream, k, NN).astype(BF16)
            gk_ref[rows, cols] = mm(upstream, q, TN).astype(BF16)
            gv_ref[rows, cols] = mm(weights_t, g, NN).astype(BF16)


def add_where(base, condition, term):
    return base + jnp.where(condition, term.astype(F32), 0.0)


def upper_bit(chip, step):
    return lax.rem(lax.div(chip, 1 << (step.bit_length() - 1)), 2)


def pair_sum_kernel(own_ref, core_ref, near_sum, *refs):
    own_state, core_state = own_ref.at[0], core_ref.at[1]
    outs = refs[-3:]
    _, chip, _, _ = places()
    state, grad = (
        (own_state[i].astype(F32) + core_state[i].astype(F32) + near_sum[i].astype(F32)).astype(BF16)
        for i in range(2)
    )
    for step, out in zip(STEPS, outs):
        out[...] = jnp.where(upper_bit(chip, step) == 0, state, grad)


def pair_scan_kernel(*refs):
    arrived = refs[:3]
    own_ref, core_ref, near_sum = refs[3:6]
    own_state, core_state = own_ref.at[0], core_ref.at[1]
    near_ref, outer_ref, wide_ref = refs[-3:]
    core, chip, low, _ = places()
    sums = [jnp.zeros(arrived[0].shape, F32)] * 2
    for step, term in zip(STEPS, arrived):
        bit = upper_bit(chip, step)
        sums = [add_where(sums[i], bit == 1 - i, term[...]) for i in range(2)]
    for i in range(2):
        own = own_state[i].astype(F32)
        other = core_state[i].astype(F32)
        near_ref[i] = add_where(sums[i], low == i, own + other).astype(BF16)
        total = add_where(sums[i], low == 1 - i, near_sum[i])
        outer_ref[i] = add_where(total, core == i, own).astype(BF16)
        wide_ref[i] = add_where(total, core == 1 - i, other).astype(BF16)


def near_scan_kernel(from_near, own_ref, core_ref, *refs):
    own_state, core_state = own_ref.at[0], core_ref.at[0]
    outer_ref, wide_ref = refs[-2:]
    core, _, _, _ = places()
    for i in range(2):
        total = from_near[i].astype(F32)
        outer_ref[i] = add_where(total, core == i, own_state[i]).astype(BF16)
        wide_ref[i] = add_where(total, core == 1 - i, core_state[i]).astype(BF16)


def block_diagonal(first, second):
    zero = jnp.zeros_like(first)
    return jnp.concatenate(
        [jnp.concatenate([first, zero], 1), jnp.concatenate([zero, second], 1)], 0
    )


def final_kernel(pairs, ready, keep, *refs):
    waiting = refs[8 * len(pairs) : 8 * len(pairs) + 3 * len(ready)]
    sems = refs[-1]
    core, _, low, quarter = places()
    half = lax.rem(core + low, 2)
    copies = []
    count = 3 * len(pairs)
    if keep:
        *outs, token = refs[-2 - count - 3 * bool(ready) : -1 - count]
    else:
        *outs, token = refs[-2 - count - 3 : -1 - count]
    buffers = refs[-1 - count : -1]
    token[...] = jnp.zeros(token.shape, token.dtype)

    def send(buffer, pair, which, row, size):
        rows = pl.ds(row, size)
        copy = pltpu.make_async_copy(
            buffer.at[rows],
            outs[which].at[rows, pair_columns(half, quarter, pair)],
            sems.at[len(copies)],
        )
        copy.start()
        copies.append(copy)

    for step, pair in enumerate(ready):
        for which in range(3):
            buffer = waiting[3 * step + which]
            send(buffer, pair, which, 0, buffer.shape[0])
    for step, pair in enumerate(pairs):
        k_ref, v_ref, g_ref, gq_in, gk_in, gv_in, wide_ref, local_ref = refs[8 * step : 8 * step + 8]
        subs = k_ref.shape[0] // SUB

        def of_sub(kind, terms):
            heads = []
            for head in range(2):
                wide = wide_ref[kind, head]
                if terms > 0:
                    wide = (
                        wide.astype(F32) + local_ref[kind, head, terms - 1].astype(F32)
                    ).astype(BF16)
                heads.append(wide)
            return block_diagonal(*heads)

        for sub in range(subs):
            rows = slice(sub * SUB, (sub + 1) * SUB)
            prefix = of_sub(0, sub)
            suffix = of_sub(1, subs - 1 - sub)
            for which, (base, rows_in, weight, dims) in enumerate(
                ((gq_in, g_ref, prefix, NT), (gk_in, v_ref, suffix, NT), (gv_in, k_ref, suffix, NN))
            ):
                buffer = buffers[3 * step + which]
                buffer[rows, :] = (
                    base[rows, :].astype(F32) + mm(rows_in[rows, :], weight, dims)
                ).astype(BF16)
                if not keep:
                    send(buffer, pair, which, sub * SUB, SUB)
    for copy in copies:
        copy.wait()


def on_device(*inputs):
    rows, width = inputs[0].shape
    count_ctx = lax.axis_size("ctx")
    factor = 1.0 / math.sqrt(HEAD * rows * count_ctx)
    subs = rows // SUB
    held = (rows, PAIR)
    square = (HEAD, HEAD)

    def swap(array, mask):
        return lax.ppermute(array, "ctx", [(i, i ^ mask) for i in range(count_ctx)])

    def states(pairs, *after):
        state, *out = call(
            lambda *refs: states_kernel(pairs, factor, *refs),
            "states_" + "_".join(map(str, pairs)),
            [(array, pltpu.HBM) for array in inputs] + [(array, pl.ANY) for array in after],
            [(VMEM, (len(pairs), 2, 2) + square)]
            + ([(VMEM, (2, 2, subs - 1) + square)] + [(VMEM, held)] * 4) * len(pairs),
            scratch=[pltpu.SemaphoreType.DMA((len(pairs), 4))],
        )
        return state, *((out[i], out[i + 1 : i + 5]) for i in range(0, len(out), 5))

    def intra(pair, arrays, after):
        return call(
            lambda *refs: intra_kernel(factor, *refs),
            f"intra_{pair}",
            [(array, VMEM) for array in arrays] + [(after, pl.ANY)],
            [(VMEM, held)] * 3,
        )

    def scan(kernel, name, args, after, count):
        return call(
            kernel,
            name,
            [(array, VMEM) for array in args] + [(array, pl.ANY) for array in after],
            count,
        )

    def final(parts, outs, ready=None, keep=False):
        ready = ready or {}
        args = []
        for arrays, partial, wide, local in parts.values():
            args += [(array, VMEM) for array in (*arrays[1:], *partial, wide, local)]
        for arrays in ready.values():
            args += [(array, VMEM) for array in arrays]
        count = len(parts)
        sends = 3 * len(ready) + (0 if keep else 3 * subs * count)
        to_outs = [(pltpu.HBM, (rows, width))] * (3 if sends else 0)
        results = [(VMEM, held)] * 3 * count
        out = call(
            lambda *refs: final_kernel(tuple(parts), tuple(ready), keep, *refs),
            "final_" + "_".join(map(str, parts)),
            args + [(array, pltpu.HBM) for array in outs],
            to_outs + [(VMEM, (16, HEAD))] + (results if keep else []),
            scratch=([] if keep else [pltpu.VMEM(held, BF16)] * 3 * count)
            + [pltpu.SemaphoreType.DMA((max(sends, 1),))],
            aliases={len(args) + i: i for i in range(len(outs))},
        )
        return out[: len(to_outs)], out[len(to_outs)], out[len(to_outs) + 1 :]

    quarter = (2, 2) + square
    state_32, (local_3, held_3), (local_2, held_2) = states((3, 2))
    core_10 = swap(state_32, 1)
    state_1, (local_1, held_1) = states((1,), state_32)
    sum_1 = (state_1[0].astype(F32) + core_10[0].astype(F32)).astype(BF16)
    near_0 = swap(sum_1, 3)
    state_0, (local_0, held_0) = states((0,), sum_1)
    partial_3 = intra(3, held_3, sum_1)
    sends = scan(
        pair_sum_kernel, "pair_sum", (state_0, core_10, near_0), partial_3, [(VMEM, (2,) + square)] * 3
    )
    arrived = [swap(array, 2 * step + step % 2) for step, array in zip(STEPS, sends)]
    partial_1 = intra(1, held_1, sends[0])
    partial_0 = intra(0, held_0, sends[0])
    for_near, outer_0, wide_0 = scan(
        pair_scan_kernel,
        "pair_scan",
        (*arrived, state_0, core_10, near_0),
        (*partial_1, *partial_0),
        [(VMEM, quarter)] * 3,
    )
    from_near = swap(for_near, 3)
    wide_2 = swap(outer_0, 1)
    partial_2 = intra(2, held_2, for_near)
    outs, token, _ = final({0: (held_0, partial_0, wide_0, local_0)}, ())
    outer_1, wide_1 = scan(
        near_scan_kernel,
        "near_scan",
        (from_near, state_1, core_10),
        (token, *partial_2),
        [(VMEM, quarter)] * 2,
    )
    wide_3 = swap(outer_1, 1)
    _, _, kept = final(
        {1: (held_1, partial_1, wide_1, local_1), 2: (held_2, partial_2, wide_2, local_2)},
        (),
        keep=True,
    )
    outs, _, _ = final(
        {3: (held_3, partial_3, wide_3, local_3)}, outs, ready={1: kept[:3], 2: kept[3:]}
    )
    return tuple(outs)


def solution(mesh):
    spec = P(("dp", "ctx"), "tp")
    return jax.shard_map(
        on_device,
        mesh=mesh,
        in_specs=(spec,) * 4,
        out_specs=(spec,) * 3,
        check_vma=False,
    )
```

```python
import math

import jax
import jax.numpy as jnp
from jax import lax
from jax.experimental import pallas as pl
from jax.experimental.pallas import tpu as pltpu
from jax.sharding import PartitionSpec as P

HEAD = 128
SUB = 256
PAIR = 2 * HEAD
F32 = jnp.float32
BF16 = jnp.bfloat16
VMEM = pltpu.VMEM
MIB = 1 << 20
STEPS = (5,7,2)

NN = (((1,), (0,)), ((), ()))
NT = (((1,), (1,)), ((), ()))
TN = (((0,), (0,)), ((), ()))


def places():
    index = lax.axis_index("ctx")
    core = lax.rem(index, 2)
    chip = lax.div(index, 2)
    low = lax.rem(chip, 2)
    quarter = lax.rem(low + lax.div(chip, 4), 2)
    return core, chip, low, quarter


def pair_columns(core, quarter, pair):
    of_core = core if pair < 2 else 1 - core
    of_quarter = quarter if pair % 2 == 0 else 1 - quarter
    return pl.ds(pl.multiple_of((2 * of_core + of_quarter) * PAIR, PAIR), PAIR)


def mm(a, b, dims):
    return lax.dot_general(a, b, dims, preferred_element_type=F32)


def call(kernel, name, args, outs, scratch=(), limit=16, aliases=None):
    def placed(array, space):
        return array if space is pl.ANY else pltpu.with_memory_space_constraint(array, space)

    out_specs = tuple(
        pl.BlockSpec(memory_space=VMEM if space is VMEM else pltpu.HBM) for space, _ in outs
    )
    out_shape = tuple(
        VMEM(shape, BF16) if space is VMEM else jax.ShapeDtypeStruct(shape, BF16)
        for space, shape in outs
    )
    return pl.pallas_call(
        kernel,
        in_specs=[pl.BlockSpec(memory_space=space) for _, space in args],
        out_specs=out_specs,
        out_shape=out_shape,
        scratch_shapes=list(scratch),
        input_output_aliases=aliases or {},
        compiler_params=pltpu.CompilerParams(vmem_limit_bytes=limit * MIB),
        cost_estimate=pl.CostEstimate(flops=0, bytes_accessed=0, transcendentals=0),
        name=name,
    )(*(placed(array, space) for array, space in args))


def states_kernel(pairs, factor, *refs):
    sources = refs[:4]
    results = refs[-5 * len(pairs) - 2 : -1]
    state_ref = results[0]
    sems = refs[-1]
    core, _, _, quarter = places()
    subs = sources[0].shape[0] // SUB

    def copy(step, which):
        return pltpu.make_async_copy(
            sources[which].at[:, pair_columns(core, quarter, pairs[step])],
            results[5 * step + 2 + which],
            sems.at[step, which],
        )

    for step in range(len(pairs)):
        for which in (1, 2, 0, 3):
            copy(step, which).start()
    for step in range(len(pairs)):
        local_ref, *held = results[5 * step + 1 : 5 * step + 6]
        for kind, (left, right) in enumerate(((1, 2), (0, 3))):
            copy(step, left).wait()
            copy(step, right).wait()
            for head in range(2):
                cols = slice(head * HEAD, (head + 1) * HEAD)
                parts = []
                for sub in range(subs):
                    rows = slice(sub * SUB, (sub + 1) * SUB)
                    parts.append(factor * mm(held[left][rows, cols], held[right][rows, cols], TN))
                if kind == 1:
                    parts = parts[::-1]
                total = parts[0]
                for sub in range(1, subs):
                    local_ref[kind, head, sub - 1] = total.astype(BF16)
                    total = total + parts[sub]
                state_ref[step, kind, head] = total.astype(BF16)


def intra_kernel(factor, q_ref, k_ref, v_ref, g_ref, _, gq_ref, gk_ref, gv_ref):
    row = lax.broadcasted_iota(jnp.int32, (SUB, SUB), 0)
    col = lax.broadcasted_iota(jnp.int32, (SUB, SUB), 1)
    subs = q_ref.shape[0] // SUB
    for head in range(2):
        cols = slice(head * HEAD, (head + 1) * HEAD)
        for sub in range(subs):
            rows = slice(sub * SUB, (sub + 1) * SUB)
            q, k, v, g = (ref[rows, cols] for ref in (q_ref, k_ref, v_ref, g_ref))
            weights_t = jnp.where(col >= row, factor * mm(k, q, NT), 0.0).astype(BF16)
            upstream = jnp.where(row >= col, factor * mm(g, v, NT), 0.0).astype(BF16)
            gq_ref[rows, cols] = mm(upstream, k, NN).astype(BF16)
            gk_ref[rows, cols] = mm(upstream, q, TN).astype(BF16)
            gv_ref[rows, cols] = mm(weights_t, g, NN).astype(BF16)


def add_where(base, condition, term):
    return base + jnp.where(condition, term.astype(F32), 0.0)


def upper_bit(chip, step):
    return lax.rem(lax.div(chip, 1 << (step.bit_length() - 1)), 2)


def pair_sum_kernel(own_ref, core_ref, near_sum, *refs):
    own_state, core_state = own_ref.at[0], core_ref.at[1]
    outs = refs[-3:]
    _, chip, _, _ = places()
    state, grad = (
        (own_state[i].astype(F32) + core_state[i].astype(F32) + near_sum[i].astype(F32)).astype(BF16)
        for i in range(2)
    )
    for step, out in zip(STEPS, outs):
        out[...] = jnp.where(upper_bit(chip, step) == 0, state, grad)


def pair_scan_kernel(*refs):
    arrived = refs[:3]
    own_ref, core_ref, near_sum = refs[3:6]
    own_state, core_state = own_ref.at[0], core_ref.at[1]
    near_ref, outer_ref, wide_ref = refs[-3:]
    core, chip, low, _ = places()
    sums = [jnp.zeros(arrived[0].shape, F32)] * 2
    for step, term in zip(STEPS, arrived):
        bit = upper_bit(chip, step)
        sums = [add_where(sums[i], bit == 1 - i, term[...]) for i in range(2)]
    for i in range(2):
        own = own_state[i].astype(F32)
        other = core_state[i].astype(F32)
        near_ref[i] = add_where(sums[i], low == i, own + other).astype(BF16)
        total = add_where(sums[i], low == 1 - i, near_sum[i])
        outer_ref[i] = add_where(total, core == i, own).astype(BF16)
        wide_ref[i] = add_where(total, core == 1 - i, other).astype(BF16)


def near_scan_kernel(from_near, own_ref, core_ref, *refs):
    own_state, core_state = own_ref.at[0], core_ref.at[0]
    outer_ref, wide_ref = refs[-2:]
    core, _, _, _ = places()
    for i in range(2):
        total = from_near[i].astype(F32)
        outer_ref[i] = add_where(total, core == i, own_state[i]).astype(BF16)
        wide_ref[i] = add_where(total, core == 1 - i, core_state[i]).astype(BF16)


def block_diagonal(first, second):
    zero = jnp.zeros_like(first)
    return jnp.concatenate(
        [jnp.concatenate([first, zero], 1), jnp.concatenate([zero, second], 1)], 0
    )


def final_kernel(pairs, ready, keep, *refs):
    waiting = refs[8 * len(pairs) : 8 * len(pairs) + 3 * len(ready)]
    sems = refs[-1]
    core, _, _, quarter = places()
    copies = []
    count = 3 * len(pairs)
    if keep:
        *outs, token = refs[-2 - count - 3 * bool(ready) : -1 - count]
    else:
        *outs, token = refs[-2 - count - 3 : -1 - count]
    buffers = refs[-1 - count : -1]
    token[...] = jnp.zeros(token.shape, token.dtype)

    def send(buffer, pair, which, row, size):
        rows = pl.ds(row, size)
        copy = pltpu.make_async_copy(
            buffer.at[rows],
            outs[which].at[rows, pair_columns(core, quarter, pair)],
            sems.at[len(copies)],
        )
        copy.start()
        copies.append(copy)

    for step, pair in enumerate(ready):
        for which in range(3):
            buffer = waiting[3 * step + which]
            send(buffer, pair, which, 0, buffer.shape[0])
    for step, pair in enumerate(pairs):
        k_ref, v_ref, g_ref, gq_in, gk_in, gv_in, wide_ref, local_ref = refs[8 * step : 8 * step + 8]
        subs = k_ref.shape[0] // SUB

        def of_sub(kind, terms):
            heads = []
            for head in range(2):
                wide = wide_ref[kind, head]
                if terms > 0:
                    wide = (
                        wide.astype(F32) + local_ref[kind, head, terms - 1].astype(F32)
                    ).astype(BF16)
                heads.append(wide)
            return block_diagonal(*heads)

        for sub in range(subs):
            rows = slice(sub * SUB, (sub + 1) * SUB)
            prefix = of_sub(0, sub)
            suffix = of_sub(1, subs - 1 - sub)
            for which, (base, rows_in, weight, dims) in enumerate(
                ((gq_in, g_ref, prefix, NT), (gk_in, v_ref, suffix, NT), (gv_in, k_ref, suffix, NN))
            ):
                buffer = buffers[3 * step + which]
                buffer[rows, :] = (
                    base[rows, :].astype(F32) + mm(rows_in[rows, :], weight, dims)
                ).astype(BF16)
                if not keep and sub == 0:
                    send(buffer, pair, which, 0, SUB)
                if not keep and sub == subs - 1:
                    send(buffer, pair, which, SUB, (subs - 1) * SUB)
    for copy in copies:
        copy.wait()


def on_device(*inputs):
    rows, width = inputs[0].shape
    count_ctx = lax.axis_size("ctx")
    factor = 1.0 / math.sqrt(HEAD * rows * count_ctx)
    subs = rows // SUB
    held = (rows, PAIR)
    square = (HEAD, HEAD)

    def swap(array, mask):
        return lax.ppermute(array, "ctx", [(i, i ^ mask) for i in range(count_ctx)])

    def states(pairs, *after):
        state, *out = call(
            lambda *refs: states_kernel(pairs, factor, *refs),
            "states_" + "_".join(map(str, pairs)),
            [(array, pltpu.HBM) for array in inputs] + [(array, pl.ANY) for array in after],
            [(VMEM, (len(pairs), 2, 2) + square)]
            + ([(VMEM, (2, 2, subs - 1) + square)] + [(VMEM, held)] * 4) * len(pairs),
            scratch=[pltpu.SemaphoreType.DMA((len(pairs), 4))],
        )
        return state, *((out[i], out[i + 1 : i + 5]) for i in range(0, len(out), 5))

    def intra(pair, arrays, after):
        return call(
            lambda *refs: intra_kernel(factor, *refs),
            f"intra_{pair}",
            [(array, VMEM) for array in arrays] + [(after, pl.ANY)],
            [(VMEM, held)] * 3,
        )

    def scan(kernel, name, args, after, count):
        return call(
            kernel,
            name,
            [(array, VMEM) for array in args] + [(array, pl.ANY) for array in after],
            count,
        )

    def final(parts, outs, ready=None, keep=False):
        ready = ready or {}
        args = []
        for arrays, partial, wide, local in parts.values():
            args += [(array, VMEM) for array in (*arrays[1:], *partial, wide, local)]
        for arrays in ready.values():
            args += [(array, VMEM) for array in arrays]
        count = len(parts)
        sends = 3 * len(ready) + (0 if keep else 6 * count)
        to_outs = [(pltpu.HBM, (rows, width))] * (3 if sends else 0)
        results = [(VMEM, held)] * 3 * count
        out = call(
            lambda *refs: final_kernel(tuple(parts), tuple(ready), keep, *refs),
            "final_" + "_".join(map(str, parts)),
            args + [(array, pltpu.HBM) for array in outs],
            to_outs + [(VMEM, (16, HEAD))] + (results if keep else []),
            scratch=([] if keep else [pltpu.VMEM(held, BF16)] * 3 * count)
            + [pltpu.SemaphoreType.DMA((max(sends, 1),))],
            aliases={len(args) + i: i for i in range(len(outs))},
        )
        return out[: len(to_outs)], out[len(to_outs)], out[len(to_outs) + 1 :]

    quarter = (2, 2) + square
    state_32, (local_3, held_3), (local_2, held_2) = states((3, 2))
    core_10 = swap(state_32, 1)
    state_1, (local_1, held_1) = states((1,), state_32)
    sum_1 = (state_1[0].astype(F32) + core_10[0].astype(F32)).astype(BF16)
    near_0 = swap(sum_1, 2)
    state_0, (local_0, held_0) = states((0,), sum_1)
    partial_3 = intra(3, held_3, sum_1)
    sends = scan(
        pair_sum_kernel, "pair_sum", (state_0, core_10, near_0), partial_3, [(VMEM, (2,) + square)] * 3
    )
    arrived = [swap(array, 2 * step) for step, array in zip(STEPS, sends)]
    partial_1 = intra(1, held_1, sends[0])
    partial_0 = intra(0, held_0, sends[0])
    for_near, outer_0, wide_0 = scan(
        pair_scan_kernel,
        "pair_scan",
        (*arrived, state_0, core_10, near_0),
        (*partial_1, *partial_0),
        [(VMEM, quarter)] * 3,
    )
    from_near = swap(for_near, 2)
    wide_2 = swap(outer_0, 1)
    partial_2 = intra(2, held_2, for_near)
    outs, token, _ = final({0: (held_0, partial_0, wide_0, local_0)}, ())
    outer_1, wide_1 = scan(
        near_scan_kernel,
        "near_scan",
        (from_near, state_1, core_10),
        (token, *partial_2),
        [(VMEM, quarter)] * 2,
    )
    wide_3 = swap(outer_1, 1)
    _, _, kept = final(
        {1: (held_1, partial_1, wide_1, local_1), 2: (held_2, partial_2, wide_2, local_2)},
        (),
        keep=True,
    )
    outs, _, _ = final(
        {3: (held_3, partial_3, wide_3, local_3)}, outs, ready={1: kept[:3], 2: kept[3:]}
    )
    return tuple(outs)


def solution(mesh):
    spec = P(("dp", "ctx"), "tp")
    return jax.shard_map(
        on_device,
        mesh=mesh,
        in_specs=(spec,) * 4,
        out_specs=(spec,) * 3,
        check_vma=False,
    )
```
